32 devices in a mesh: groups: 2 (over x), feat: 16 (over z, y, core).
Axes of the slice: x: 2, y: 2, z: 4, core: 2. Of those that a mesh axis runs over, the one named last changes fastest.
Arguments:
- samples: bfloat16 [4096, 512], P(('groups', 'feat')), parts along dimension 0, may hold values from -0.26367188 to 0.26367188
- targets: bfloat16 [4096, 256], P(('groups', 'feat')), parts along dimension 0, may hold values from -6 to 6
- frequencies: bfloat16 [512, 32768], P(None, 'feat'), may hold values from -6 to 6
- phases: float32 [32768], P('feat'), may hold values from -3.140625 to 3.140625
- coefficients: float32 [32768, 512], P('feat', 'groups'), parts along dimension 1, may hold values from -6 to 6
- eigenbasis: bfloat16 [32768, 256], P('feat', 'groups'), parts along dimension 1, may hold values from -0.03125 to 0.03125
- eigenvalues: float32 [256], P('groups'), parts along dimension 0, may hold values from 1 to 100
Outputs:
- new_coefficients: float32 [32768, 512], P('feat', 'groups'), parts along dimension 1
- scaled_projection: float32 [256, 256], P('groups'), parts along dimension 0
The draws below stay inside these ranges and needn't reach their ends.
There are 2 independent parts, one for each index of `groups`. The reference program is written for one: setup_inputs(seed, part) draws one part's arguments, and reference() takes and returns one part's arrays. A program takes and returns all parts, laid end to end along the dimension named above; an argument that names none is the same for every part. Nothing has to cross between parts.
All inputs are finite; a program needn't handle non-finite values.
Results may differ from the reference program's by a relative error of at most 0.005.
Values may be sent and summed in bfloat16 or wider, within the bound.
A program may use at most 128 MiB of HBM per device.

```python
import math
import jax
import jax.numpy as jnp
from jax import lax

DIN = 512
OUT = 256
TOPK = 128
STEPS = 2
M = 32768
B = 2048


def level_of(stream_key, dims, split, smallest, high):
    level = 1.0
    for position, blocks in split:
        heights = jax.random.uniform(jax.random.fold_in(jax.random.fold_in(stream_key, 6), position), (blocks,), jnp.float32, smallest / len(split), high / len(split))
        level = level * jnp.repeat(jnp.exp(heights), dims[position] // blocks).reshape((-1,) + (1,) * (len(dims) - 1 - position))
    return level


def scatter_about(key, shape, deviation, bound, cuts=(), kind=jnp.bfloat16):
    array = jax.random.normal(key, shape, jnp.float32) * deviation
    if len(cuts) > 0:
        array = level_of(key, shape, cuts, -0.22, 0.18) * array
    return jnp.clip(array, min=-bound, max=bound).astype(kind)


def setup_inputs(seed: int = 0, part: int = 0) -> dict:
    splits = jax.random.split(jax.random.key(seed), 8)
    own_keys = jax.random.split(jax.random.fold_in(splits[7], part), 8)
    return {
        "samples": scatter_about(own_keys[0], (B, DIN), (DIN ** -0.5), 0.26367188, ((0, 16),)),
        "targets": scatter_about(own_keys[1], (B, OUT), 1.0, 6.0, ((0, 16),)),
        "frequencies": scatter_about(splits[2], (DIN, M), 1.0, 6.0, ((1, 16),)),
        "phases": jnp.clip(jax.random.uniform(splits[3], (M,), jnp.float32, -3.140625, 3.140625), -3.140625, 3.140625),
        "coefficients": scatter_about(own_keys[4], (M, OUT), 1.0, 6.0, ((0, 16),), jnp.float32),
        "eigenbasis": scatter_about(own_keys[5], (M, TOPK), M ** -0.5, 0.03125, ((0, 16),)),
        "eigenvalues": jnp.clip(jnp.exp(jax.random.uniform(own_keys[6], (TOPK,), jnp.float32, math.log(1.0), math.log(100.0))), 1.0, 100.0),
    }


def featurize(samples, frequencies, phases):
    product = jnp.dot(samples, frequencies, preferred_element_type=jnp.float32)
    index = jnp.arange(M, dtype=jnp.int32).astype(jnp.float32)
    sweep = jnp.exp(jnp.log(8.0) * index / M)
    return jnp.cos(product * sweep[None, :] + phases[None, :]).astype(jnp.bfloat16)

def reference(samples, targets, frequencies, phases, coefficients, eigenbasis, eigenvalues):
    features = featurize(samples, frequencies, phases)
    retained = 1.0 - 1.0 / eigenvalues
    step_rate = 0.5 * jnp.sqrt(jnp.float32(B) / jnp.float32(M))
    basis_wide = eigenbasis.astype(jnp.float32)
    current = coefficients
    scaled = jnp.zeros((TOPK, OUT), jnp.float32)
    for iteration in range(STEPS):
        current_low = current.astype(jnp.bfloat16)
        prediction = jnp.dot(features, current_low, preferred_element_type=jnp.float32) / jnp.sqrt(jnp.float32(M))
        residual = (prediction - targets.astype(jnp.float32)).astype(jnp.bfloat16)
        gradient = lax.dot_general(features, residual, (((0,), (0,)), ((), ())), preferred_element_type=jnp.float32) / jnp.sqrt(jnp.float32(B))
        projected = jnp.dot(basis_wide.T, gradient, precision=lax.Precision.HIGHEST)
        scaled = retained[:, None] * projected
        correction = jnp.dot(basis_wide, scaled, precision=lax.Precision.HIGHEST)
        current = current - step_rate * (gradient - correction)
    return (current, scaled)
```

```python
import functools
import math

import jax
import jax.numpy as jnp
from jax import lax
from jax.experimental import pallas as pl
from jax.experimental.pallas import tpu as pltpu
from jax.sharding import PartitionSpec as P

STEPS = 2
F32 = jnp.float32
BF16 = jnp.bfloat16
COSINE = (
    0.9999991998413434, -19.738978175861273, 64.92858783993262,
    -85.27084362689533, 58.786940762944745, -21.065429407375632,
)
TN_DIMS = (((0,), (0,)), ((), ()))


def tn_dot(left, right):
    return lax.dot_general(left, right, TN_DIMS, preferred_element_type=F32)


class Gather:
    def __init__(self, place, buf, rows, recv, send):
        self.place, self.buf, self.rows, self.recv, self.send = place, buf, rows, recv, send

    def copy(self, chunk, slot, target):
        part = self.buf.at[pl.ds(pl.multiple_of(chunk * self.rows, self.rows), self.rows)]
        return pltpu.make_async_remote_copy(
            src_ref=part,
            dst_ref=part,
            send_sem=self.send.at[slot],
            recv_sem=self.recv.at[chunk],
            device_id={"feat": target},
            device_id_type=pl.DeviceIdType.MESH,
        )

    def arrived(self, chunk):
        self.copy(chunk, 0, self.place.sibling).wait_recv()

    def line_copies(self, k):
        s = self.place
        chunk = s.chunk(k, s.y, s.c)
        right = (s.q + 1 < s.zn) if k == 0 else jnp.logical_and(s.order[k] < s.q, s.q + 1 < s.zn)
        left = (s.q > 0) if k == 0 else jnp.logical_and(s.order[k] > s.q, s.q > 0)
        return (
            (right, self.copy(chunk, 5 * k, s.device(jnp.minimum(s.q + 1, s.zn - 1), s.y, s.c))),
            (left, self.copy(chunk, 5 * k + 1, s.device(jnp.maximum(s.q - 1, 0), s.y, s.c))),
        )

    def near_copies(self, k):
        s = self.place
        chunk = s.chunk(k, s.y, s.c)
        return (self.copy(chunk, 5 * k + 2, s.partner), self.copy(chunk, 5 * k + 3, s.sibling))

    def cross_copy(self, k):
        s = self.place
        return self.copy(s.chunk(k, 1 - s.y, s.c), 5 * k + 4, s.sibling)

    def forward(self, k):
        s = self.place
        if k > 0:
            self.arrived(s.chunk(k, s.y, s.c))
        for needed, copy in self.line_copies(k):
            pl.when(needed)(copy.start)
        for copy in self.near_copies(k):
            copy.start()

    def cross(self, k):
        s = self.place
        self.arrived(s.chunk(k, 1 - s.y, s.c))
        self.cross_copy(k).start()

    def near_half(self, k):
        s = self.place
        self.arrived(s.chunk(k, s.y, 1 - s.c))

    def far_half(self, k):
        s = self.place
        self.arrived(s.chunk(k, 1 - s.y, 1 - s.c))

    def finish(self):
        for k in range(self.place.zn):
            for needed, copy in self.line_copies(k):
                pl.when(needed)(copy.wait_send)
            for copy in self.near_copies(k):
                copy.wait_send()
            self.cross_copy(k).wait_send()


class Scatter:
    def __init__(self, place, rows, keep, core, side, line, core_sem, side_sem, line_sem):
        self.place, self.rows = place, rows
        self.keep = keep
        self.core_out, self.core_in = core
        self.side_out, self.side_in = side
        self.line_out, self.line_in = line
        self.core_sem, self.side_sem, self.line_sem = core_sem, side_sem, line_sem

    def core_copy(self, slot):
        return pltpu.make_async_remote_copy(
            src_ref=self.core_out.at[slot],
            dst_ref=self.core_in.at[slot],
            send_sem=self.core_sem.at[0, slot],
            recv_sem=self.core_sem.at[1, slot],
            device_id={"feat": self.place.sibling},
            device_id_type=pl.DeviceIdType.MESH,
        )

    def side_copy(self, k):
        return pltpu.make_async_remote_copy(
            src_ref=self.side_out.at[k],
            dst_ref=self.side_in.at[k],
            send_sem=self.side_sem.at[0, k],
            recv_sem=self.side_sem.at[1, k],
            device_id={"feat": self.place.partner},
            device_id_type=pl.DeviceIdType.MESH,
        )

    def line_copy(self, k):
        s = self.place
        return pltpu.make_async_remote_copy(
            src_ref=self.line_out.at[k],
            dst_ref=self.line_in.at[s.q],
            send_sem=self.line_sem.at[0, k],
            recv_sem=self.line_sem.at[1, s.q],
            device_id={"feat": s.device(s.order[k], s.y, s.c)},
            device_id_type=pl.DeviceIdType.MESH,
        )

    def line_arrival(self, k):
        s = self.place
        other = s.order[k]
        return pltpu.make_async_remote_copy(
            src_ref=self.line_out.at[k],
            dst_ref=self.line_in.at[other],
            send_sem=self.line_sem.at[0, k],
            recv_sem=self.line_sem.at[1, other],
            device_id={"feat": s.device(other, s.y, s.c)},
            device_id_type=pl.DeviceIdType.MESH,
        )

    def put(self, k, far, sums):
        slot = 2 * k + far
        self.keep[slot] = sums(self.place.c)
        self.core_out[slot] = sums(1 - self.place.c).astype(BF16)
        self.core_copy(slot).start()

    def merge_core(self, k, far):
        slot = 2 * k + far
        self.core_copy(slot).wait_recv()
        total = self.keep[slot] + self.core_in[slot].astype(F32)
        if far:
            self.side_out[k] = total.astype(BF16)
            self.side_copy(k).start()
        else:
            self.keep[slot] = total

    def merge_side(self, k):
        self.side_copy(k).wait_recv()
        total = self.keep[2 * k] + self.side_in[k].astype(F32)
        if k:
            self.line_out[k] = total.astype(BF16)
            self.line_copy(k).start()
        else:
            self.keep[0] = total

    def result(self):
        total = self.keep[0]
        for k in range(1, self.place.zn):
            self.line_arrival(k).wait_recv()
            total = total + self.line_in[self.place.order[k]].astype(F32)
        return total

    def finish(self):
        for k in range(self.place.zn):
            self.core_copy(2 * k).wait_send()
            self.core_copy(2 * k + 1).wait_send()
            self.side_copy(k).wait_send()
            if k:
                self.line_copy(k).wait_send()


class Place:
    def __init__(self, size):
        self.zn = zn = size // 4
        me = lax.axis_index("feat")
        self.me = me
        self.q = q = me // 4
        self.y = (me // 2) % 2
        self.c = me % 2
        near = jnp.minimum(q, zn - 1 - q)
        self.order = []
        for k in range(zn):
            step = -((k + 1) // 2) if k % 2 else k // 2
            edge = jnp.where(q == near, k, zn - 1 - k)
            self.order.append(jnp.where(k <= 2 * near, q + step, edge))
        self.sibling = self.device(q, self.y, 1 - self.c)
        self.partner = self.device(q, 1 - self.y, self.c)

    def device(self, q, y, c):
        return (q * 2 + y) * 2 + c

    def chunk(self, k, y, c):
        return self.device(self.order[k], y, c)


def kernel(
    size, total_feat,
    x_ref, y_ref, w_ref, phase_ref, a_ref, e_ref, eig_ref,
    out_ref, scaled_ref,
    xs, feats, spread, joint, low, grad, part, res1, res2,
    keep1, core_out1, core_in1, side_out1, side_in1, line_out1, line_in1,
    keep2, core_out2, core_in2, side_out2, side_in2, line_out2, line_in2,
    g_recv, g_send, s_core, s_side, s_line,
):
    place = Place(size)
    zn = place.zn
    rows = x_ref.shape[0]
    feat_dev = w_ref.shape[1]
    outs = a_ref.shape[1]
    top = e_ref.shape[1]
    tile = min(256, feat_dev)
    tiles = feat_dev // tile
    total_rows = rows * size
    step_rate = 0.5 * math.sqrt(total_rows / total_feat)
    feature_norm = 1.0 / math.sqrt(total_feat)
    sample_norm = 1.0 / math.sqrt(total_rows)

    barrier = pltpu.get_barrier_semaphore()
    others = [place.sibling, place.partner] + [
        place.device(place.order[k], place.y, place.c) for k in range(1, zn)
    ]
    for other in others:
        pl.semaphore_signal(
            barrier, inc=1, device_id={"feat": other}, device_id_type=pl.DeviceIdType.MESH
        )

    own = pl.ds(pl.multiple_of(place.me * rows, rows), rows)
    xs[own, :] = x_ref[...]
    pl.semaphore_wait(barrier, len(others))
    gather_x = Gather(place, xs, rows, g_recv.at[0], g_send.at[0])
    gather_x.forward(0)

    index = (place.me * feat_dev + lax.broadcasted_iota(jnp.int32, (8, feat_dev), 1)).astype(F32)
    turn = 1.0 / (2.0 * math.pi)
    sweep = jnp.exp(F32(math.log(8.0)) * index / F32(total_feat))
    spread[0:8, :] = sweep * turn
    spread[8:16, :] = jnp.broadcast_to(phase_ref[...] * turn, (8, feat_dev))
    joint[:, :outs] = a_ref[...].astype(BF16)
    joint[:, outs:] = e_ref[...]

    pair = 2 * rows

    def pair_rows(k, far):
        y = 1 - place.y if far else place.y
        first = (place.order[k] * 2 + y) * pair
        return pl.ds(pl.multiple_of(first, pair), pair)

    def make_features(span):
        def body(i, carry):
            cols = pl.ds(pl.multiple_of(i * tile, tile), tile)
            product = jnp.dot(xs[span, :], w_ref[:, cols], preferred_element_type=F32)
            turns = product * spread[0:1, cols] + spread[8:9, cols]
            f = turns - jnp.round(turns)
            u = f * f
            value = jnp.full_like(u, COSINE[-1])
            for coefficient in COSINE[-2::-1]:
                value = value * u + coefficient
            feats[span, cols] = value.astype(BF16)
            return carry

        lax.fori_loop(0, tiles, body, 0, unroll=2)

    def predict(span, factors, scatter, k, far, columns):
        part[:, :columns] = jnp.dot(feats[span, :], factors[...], preferred_element_type=F32)

        def sums(core):
            return part[pl.ds(pl.multiple_of(core * rows, rows), rows), :columns]

        scatter.put(k, far, sums)

    scatter1 = Scatter(
        place, rows, keep1, (core_out1, core_in1), (side_out1, side_in1), (line_out1, line_in1),
        s_core.at[0], s_side.at[0], s_line.at[0],
    )
    scatter2 = Scatter(
        place, rows, keep2, (core_out2, core_in2), (side_out2, side_in2), (line_out2, line_in2),
        s_core.at[1], s_side.at[1], s_line.at[1],
    )

    for k in range(zn):
        gather_x.near_half(k)
        make_features(pair_rows(k, 0))
        gather_x.cross(k)
        if k + 1 < zn:
            gather_x.forward(k + 1)
        predict(pair_rows(k, 0), joint, scatter1, k, 0, outs + top)
        if k:
            scatter1.merge_core(k - 1, 1)
        gather_x.far_half(k)
        make_features(pair_rows(k, 1))
        scatter1.merge_core(k, 0)
        predict(pair_rows(k, 1), joint, scatter1, k, 1, outs + top)
        if k:
            scatter1.merge_side(k - 1)
    scatter1.merge_core(zn - 1, 1)
    scatter1.merge_side(zn - 1)

    total = scatter1.result()
    prediction = total[:, :outs] * feature_norm
    res1[own, :outs] = (prediction - y_ref[...].astype(F32)).astype(BF16)
    res1[own, outs:] = total[:, outs:].astype(BF16)

    eig = jnp.broadcast_to(1.0 - 1.0 / eig_ref[...], (top, top))
    same = lax.broadcasted_iota(jnp.int32, (top, top), 0) == lax.broadcasted_iota(
        jnp.int32, (top, top), 1
    )
    retained = jnp.sum(jnp.where(same, eig, 0.0), axis=1, keepdims=True)

    def descend(gather, res, source):
        quad = 4 * rows
        projected = jnp.zeros((top, outs), F32)
        gather.forward(0)
        for k in range(zn):
            gather.cross(k)
            if k + 1 < zn:
                gather.forward(k + 1)
            gather.near_half(k)
            gather.far_half(k)
            span = pl.ds(pl.multiple_of(place.order[k] * quad, quad), quad)

            def body(i, carry):
                cols = pl.ds(pl.multiple_of(i * tile, tile), tile)
                term = tn_dot(feats[span, cols], res[span, :outs])
                grad[cols, :] = term if k == 0 else grad[cols, :] + term
                return carry

            lax.fori_loop(0, tiles, body, 0)
            projected = projected + tn_dot(res1[span, outs:], res[span, :outs])
        scaled = retained * (projected * sample_norm)
        upper = scaled.astype(BF16)
        lower = (scaled - upper.astype(F32)).astype(BF16)

        def update(i, carry):
            cols = pl.ds(pl.multiple_of(i * tile, tile), tile)
            basis = e_ref[cols, :]
            correction = jnp.dot(basis, upper, preferred_element_type=F32) + jnp.dot(
                basis, lower, preferred_element_type=F32
            )
            new = source[cols, :] - step_rate * (grad[cols, :] * sample_norm - correction)
            out_ref[cols, :] = new
            low[cols, :] = new.astype(BF16)
            return carry

        lax.fori_loop(0, tiles, update, 0)
        return scaled

    gather1 = Gather(place, res1, rows, g_recv.at[1], g_send.at[1])
    descend(gather1, res1, a_ref)

    for k in reversed(range(zn)):
        for far in (1, 0):
            predict(pair_rows(k, far), low, scatter2, k, far, outs)
        if k + 1 < zn:
            scatter2.merge_core(k + 1, 1)
            scatter2.merge_core(k + 1, 0)
        if k + 2 < zn:
            scatter2.merge_side(k + 2)
    scatter2.merge_core(0, 1)
    scatter2.merge_core(0, 0)
    scatter2.merge_side(1)
    scatter2.merge_side(0)
    prediction = scatter2.result() * feature_norm
    res2[own, :] = (prediction - y_ref[...].astype(F32)).astype(BF16)
    gather2 = Gather(place, res2, rows, g_recv.at[2], g_send.at[2])
    scaled_ref[...] = descend(gather2, res2, out_ref)

    for transfer in (gather_x, scatter1, gather1, scatter2, gather2):
        transfer.finish()


def local(samples, targets, frequencies, phases, coefficients, eigenbasis, eigenvalues):
    size = lax.axis_size("feat")
    rows, din = samples.shape
    feat_dev = frequencies.shape[1]
    outs = coefficients.shape[1]
    top = eigenbasis.shape[1]
    zn = size // 4
    wide = outs + top
    total_rows = rows * size

    def scatter_buffers(columns):
        return [
            pltpu.VMEM((2 * zn, rows, columns), F32),
            pltpu.VMEM((2 * zn, rows, columns), BF16),
            pltpu.VMEM((2 * zn, rows, columns), BF16),
            pltpu.VMEM((zn, rows, columns), BF16),
            pltpu.VMEM((zn, rows, columns), BF16),
            pltpu.VMEM((zn, rows, columns), BF16),
            pltpu.VMEM((zn, rows, columns), BF16),
        ]

    vmem = pl.BlockSpec(memory_space=pltpu.VMEM)
    return pl.pallas_call(
        functools.partial(kernel, size, feat_dev * size),
        out_shape=(
            jax.ShapeDtypeStruct(coefficients.shape, F32),
            jax.ShapeDtypeStruct((top, outs), F32),
        ),
        in_specs=[vmem] * 7,
        out_specs=(vmem, vmem),
        scratch_shapes=[
            pltpu.VMEM((total_rows, din), BF16),
            pltpu.VMEM((total_rows, feat_dev), BF16),
            pltpu.VMEM((16, feat_dev), F32),
            pltpu.VMEM((feat_dev, wide), BF16),
            pltpu.VMEM((feat_dev, outs), BF16),
            pltpu.VMEM((feat_dev, outs), F32),
            pltpu.VMEM((2 * rows, wide), F32),
            pltpu.VMEM((total_rows, wide), BF16),
            pltpu.VMEM((total_rows, outs), BF16),
            *scatter_buffers(wide),
            *scatter_buffers(outs),
            pltpu.SemaphoreType.DMA((3, size)),
            pltpu.SemaphoreType.DMA((3, 5 * zn)),
            pltpu.SemaphoreType.DMA((2, 2, 2 * zn)),
            pltpu.SemaphoreType.DMA((2, 2, zn)),
            pltpu.SemaphoreType.DMA((2, 2, zn)),
        ],
        compiler_params=pltpu.CompilerParams(
            collective_id=0, has_side_effects=True, vmem_limit_bytes=60 * 1024 * 1024
        ),
    )(
        samples, targets, frequencies, phases.reshape(1, feat_dev), coefficients, eigenbasis,
        eigenvalues.reshape(1, top),
    )


def solution(mesh):
    return jax.shard_map(
        local,
        mesh=mesh,
        in_specs=(
            P(("groups", "feat"), None),
            P(("groups", "feat"), None),
            P(None, "feat"),
            P("feat"),
            P("feat", "groups"),
            P("feat", "groups"),
            P("groups"),
        ),
        out_specs=(P("feat", "groups"), P("groups", None)),
        check_vma=False,
    )
```

```python
import functools
import math

import jax
import jax.numpy as jnp
from jax import lax
from jax.experimental import pallas as pl
from jax.experimental.pallas import tpu as pltpu
from jax.sharding import PartitionSpec as P

STEPS = 2
F32 = jnp.float32
BF16 = jnp.bfloat16
COSINE = (
    0.9999991998413434, -19.738978175861273, 64.92858783993262,
    -85.27084362689533, 58.786940762944745, -21.065429407375632,
)
TN_DIMS = (((0,), (0,)), ((), ()))


def tn_dot(left, right):
    return lax.dot_general(left, right, TN_DIMS, preferred_element_type=F32)


class Gather:
    def __init__(self, place, buf, rows, recv, send):
        self.place, self.buf, self.rows, self.recv, self.send = place, buf, rows, recv, send

    def copy(self, chunk, slot, target):
        part = self.buf.at[pl.ds(pl.multiple_of(chunk * self.rows, self.rows), self.rows)]
        return pltpu.make_async_remote_copy(
            src_ref=part,
            dst_ref=part,
            send_sem=self.send.at[slot],
            recv_sem=self.recv.at[chunk],
            device_id={"feat": target},
            device_id_type=pl.DeviceIdType.MESH,
        )

    def arrived(self, chunk):
        self.copy(chunk, 0, self.place.sibling).wait_recv()

    def line_copies(self, k):
        s = self.place
        chunk = s.chunk(k, s.y, s.c)
        right = (s.q + 1 < s.zn) if k == 0 else jnp.logical_and(s.order[k] < s.q, s.q + 1 < s.zn)
        left = (s.q > 0) if k == 0 else jnp.logical_and(s.order[k] > s.q, s.q > 0)
        return (
            (right, self.copy(chunk, 5 * k, s.device(jnp.minimum(s.q + 1, s.zn - 1), s.y, s.c))),
            (left, self.copy(chunk, 5 * k + 1, s.device(jnp.maximum(s.q - 1, 0), s.y, s.c))),
        )

    def near_copies(self, k):
        s = self.place
        chunk = s.chunk(k, s.y, s.c)
        return (self.copy(chunk, 5 * k + 2, s.partner), self.copy(chunk, 5 * k + 3, s.sibling))

    def cross_copy(self, k):
        s = self.place
        return self.copy(s.chunk(k, 1 - s.y, s.c), 5 * k + 4, s.sibling)

    def forward(self, k):
        s = self.place
        if k > 0:
            self.arrived(s.chunk(k, s.y, s.c))
        for needed, copy in self.line_copies(k):
            pl.when(needed)(copy.start)
        for copy in self.near_copies(k):
            copy.start()

    def cross(self, k):
        s = self.place
        self.arrived(s.chunk(k, 1 - s.y, s.c))
        self.cross_copy(k).start()

    def near_half(self, k):
        s = self.place
        self.arrived(s.chunk(k, s.y, 1 - s.c))

    def far_half(self, k):
        s = self.place
        self.arrived(s.chunk(k, 1 - s.y, 1 - s.c))

    def finish(self):
        for k in range(self.place.zn):
            for needed, copy in self.line_copies(k):
                pl.when(needed)(copy.wait_send)
            for copy in self.near_copies(k):
                copy.wait_send()
            self.cross_copy(k).wait_send()


class Scatter:
    def __init__(self, place, rows, keep, core, side, line, core_sem, side_sem, line_sem):
        self.place, self.rows = place, rows
        self.keep = keep
        self.core_out, self.core_in = core
        self.side_out, self.side_in = side
        self.line_out, self.line_in = line
        self.core_sem, self.side_sem, self.line_sem = core_sem, side_sem, line_sem

    def core_copy(self, slot):
        return pltpu.make_async_remote_copy(
            src_ref=self.core_out.at[slot],
            dst_ref=self.core_in.at[slot],
            send_sem=self.core_sem.at[0, slot],
            recv_sem=self.core_sem.at[1, slot],
            device_id={"feat": self.place.sibling},
            device_id_type=pl.DeviceIdType.MESH,
        )

    def side_copy(self, k):
        return pltpu.make_async_remote_copy(
            src_ref=self.side_out.at[k],
            dst_ref=self.side_in.at[k],
            send_sem=self.side_sem.at[0, k],
            recv_sem=self.side_sem.at[1, k],
            device_id={"feat": self.place.partner},
            device_id_type=pl.DeviceIdType.MESH,
        )

    def line_copy(self, k):
        s = self.place
        return pltpu.make_async_remote_copy(
            src_ref=self.line_out.at[k],
            dst_ref=self.line_in.at[s.q],
            send_sem=self.line_sem.at[0, k],
            recv_sem=self.line_sem.at[1, s.q],
            device_id={"feat": s.device(s.order[k], s.y, s.c)},
            device_id_type=pl.DeviceIdType.MESH,
        )

    def line_arrival(self, k):
        s = self.place
        other = s.order[k]
        return pltpu.make_async_remote_copy(
            src_ref=self.line_out.at[k],
            dst_ref=self.line_in.at[other],
            send_sem=self.line_sem.at[0, k],
            recv_sem=self.line_sem.at[1, other],
            device_id={"feat": s.device(other, s.y, s.c)},
            device_id_type=pl.DeviceIdType.MESH,
        )

    def put(self, k, far, sums):
        slot = 2 * k + far
        self.keep[slot] = sums(self.place.c)
        self.core_out[slot] = sums(1 - self.place.c).astype(BF16)
        self.core_copy(slot).start()

    def merge_core(self, k, far):
        slot = 2 * k + far
        self.core_copy(slot).wait_recv()
        total = self.keep[slot] + self.core_in[slot].astype(F32)
        if far:
            self.side_out[k] = total.astype(BF16)
            self.side_copy(k).start()
        else:
            self.keep[slot] = total

    def merge_side(self, k):
        self.side_copy(k).wait_recv()
        total = self.keep[2 * k] + self.side_in[k].astype(F32)
        if k:
            self.line_out[k] = total.astype(BF16)
            self.line_copy(k).start()
        else:
            self.keep[0] = total

    def result(self):
        total = self.keep[0]
        for k in range(1, self.place.zn):
            self.line_arrival(k).wait_recv()
            total = total + self.line_in[self.place.order[k]].astype(F32)
        return total

    def finish(self):
        for k in range(self.place.zn):
            self.core_copy(2 * k).wait_send()
            self.core_copy(2 * k + 1).wait_send()
            self.side_copy(k).wait_send()
            if k:
                self.line_copy(k).wait_send()


class Place:
    def __init__(self, size):
        self.zn = zn = size // 4
        me = lax.axis_index("feat")
        self.me = me
        self.q = q = me // 4
        self.y = (me // 2) % 2
        self.c = me % 2
        near = jnp.minimum(q, zn - 1 - q)
        self.order = []
        for k in range(zn):
            step = -((k + 1) // 2) if k % 2 else k // 2
            edge = jnp.where(q == near, k, zn - 1 - k)
            self.order.append(jnp.where(k <= 2 * near, q + step, edge))
        self.sibling = self.device(q, self.y, 1 - self.c)
        self.partner = self.device(q, 1 - self.y, self.c)

    def device(self, q, y, c):
        return (q * 2 + y) * 2 + c

    def chunk(self, k, y, c):
        return self.device(self.order[k], y, c)


def kernel(
    size, total_feat,
    x_ref, y_ref, w_ref, phase_ref, a_ref, e_ref, eig_ref,
    out_ref, scaled_ref,
    xs, feats, spread, joint, low, grad, part, res1, res2,
    keep1, core_out1, core_in1, side_out1, side_in1, line_out1, line_in1,
    keep2, core_out2, core_in2, side_out2, side_in2, line_out2, line_in2,
    g_recv, g_send, s_core, s_side, s_line,
):
    place = Place(size)
    zn = place.zn
    rows = x_ref.shape[0]
    feat_dev = w_ref.shape[1]
    outs = a_ref.shape[1]
    top = e_ref.shape[1]
    tile = min(256, feat_dev)
    tiles = feat_dev // tile
    total_rows = rows * size
    step_rate = 0.5 * math.sqrt(total_rows / total_feat)
    feature_norm = 1.0 / math.sqrt(total_feat)
    sample_norm = 1.0 / math.sqrt(total_rows)

    barrier = pltpu.get_barrier_semaphore()
    others = [place.sibling, place.partner] + [
        place.device(place.order[k], place.y, place.c) for k in range(1, zn)
    ]
    for other in others:
        pl.semaphore_signal(
            barrier, inc=1, device_id={"feat": other}, device_id_type=pl.DeviceIdType.MESH
        )

    own = pl.ds(pl.multiple_of(place.me * rows, rows), rows)
    xs[own, :] = x_ref[...]
    pl.semaphore_wait(barrier, len(others))
    gather_x = Gather(place, xs, rows, g_recv.at[0], g_send.at[0])
    gather_x.forward(0)

    index = (place.me * feat_dev + lax.broadcasted_iota(jnp.int32, (8, feat_dev), 1)).astype(F32)
    turn = 1.0 / (2.0 * math.pi)
    sweep = jnp.exp(F32(math.log(8.0)) * index / F32(total_feat))
    spread[0:8, :] = sweep * turn
    spread[8:16, :] = jnp.broadcast_to(phase_ref[...] * turn, (8, feat_dev))
    joint[:, :outs] = a_ref[...].astype(BF16)
    joint[:, outs:] = e_ref[...]

    pair = 2 * rows

    def pair_rows(k, far):
        y = 1 - place.y if far else place.y
        first = (place.order[k] * 2 + y) * pair
        return pl.ds(pl.multiple_of(first, pair), pair)

    def make_features(span):
        def body(i, carry):
            cols = pl.ds(pl.multiple_of(i * tile, tile), tile)
            product = jnp.dot(xs[span, :], w_ref[:, cols], preferred_element_type=F32)
            turns = product * spread[0:1, cols] + spread[8:9, cols]
            f = turns - jnp.round(turns)
            u = f * f
            value = jnp.full_like(u, COSINE[-1])
            for coefficient in COSINE[-2::-1]:
                value = value * u + coefficient
            feats[span, cols] = value.astype(BF16)
            return carry

        lax.fori_loop(0, tiles, body, 0, unroll=True)

    def predict(span, factors, scatter, k, far, columns):
        part[:, :columns] = jnp.dot(feats[span, :], factors[...], preferred_element_type=F32)

        def sums(core):
            return part[pl.ds(pl.multiple_of(core * rows, rows), rows), :columns]

        scatter.put(k, far, sums)

    scatter1 = Scatter(
        place, rows, keep1, (core_out1, core_in1), (side_out1, side_in1), (line_out1, line_in1),
        s_core.at[0], s_side.at[0], s_line.at[0],
    )
    scatter2 = Scatter(
        place, rows, keep2, (core_out2, core_in2), (side_out2, side_in2), (line_out2, line_in2),
        s_core.at[1], s_side.at[1], s_line.at[1],
    )

    for k in range(zn):
        gather_x.near_half(k)
        make_features(pair_rows(k, 0))
        gather_x.cross(k)
        if k + 1 < zn:
            gather_x.forward(k + 1)
        predict(pair_rows(k, 0), joint, scatter1, k, 0, outs + top)
        if k:
            scatter1.merge_core(k - 1, 1)
        gather_x.far_half(k)
        make_features(pair_rows(k, 1))
        scatter1.merge_core(k, 0)
        predict(pair_rows(k, 1), joint, scatter1, k, 1, outs + top)
        if k:
            scatter1.merge_side(k - 1)
    scatter1.merge_core(zn - 1, 1)
    scatter1.merge_side(zn - 1)

    total = scatter1.result()
    prediction = total[:, :outs] * feature_norm
    res1[own, :outs] = (prediction - y_ref[...].astype(F32)).astype(BF16)
    res1[own, outs:] = total[:, outs:].astype(BF16)

    eig = jnp.broadcast_to(1.0 - 1.0 / eig_ref[...], (top, top))
    same = lax.broadcasted_iota(jnp.int32, (top, top), 0) == lax.broadcasted_iota(
        jnp.int32, (top, top), 1
    )
    retained = jnp.sum(jnp.where(same, eig, 0.0), axis=1, keepdims=True)

    def descend(gather, res, source):
        quad = 4 * rows
        projected = jnp.zeros((top, outs), F32)
        gather.forward(0)
        for k in range(zn):
            gather.cross(k)
            if k + 1 < zn:
                gather.forward(k + 1)
            gather.near_half(k)
            gather.far_half(k)
            span = pl.ds(pl.multiple_of(place.order[k] * quad, quad), quad)

            def body(i, carry):
                cols = pl.ds(pl.multiple_of(i * tile, tile), tile)
                term = tn_dot(feats[span, cols], res[span, :outs])
                grad[cols, :] = term if k == 0 else grad[cols, :] + term
                return carry

            lax.fori_loop(0, tiles, body, 0, unroll=True)
            projected = projected + tn_dot(res1[span, outs:], res[span, :outs])
        scaled = retained * (projected * sample_norm)
        upper = scaled.astype(BF16)
        lower = (scaled - upper.astype(F32)).astype(BF16)

        def update(i, carry):
            cols = pl.ds(pl.multiple_of(i * tile, tile), tile)
            basis = e_ref[cols, :]
            correction = jnp.dot(basis, upper, preferred_element_type=F32) + jnp.dot(
                basis, lower, preferred_element_type=F32
            )
            new = source[cols, :] - step_rate * (grad[cols, :] * sample_norm - correction)
            out_ref[cols, :] = new
            low[cols, :] = new.astype(BF16)
            return carry

        lax.fori_loop(0, tiles, update, 0)
        return scaled

    gather1 = Gather(place, res1, rows, g_recv.at[1], g_send.at[1])
    descend(gather1, res1, a_ref)

    for k in reversed(range(zn)):
        for far in (1, 0):
            predict(pair_rows(k, far), low, scatter2, k, far, outs)
        if k + 1 < zn:
            scatter2.merge_core(k + 1, 1)
            scatter2.merge_core(k + 1, 0)
        if k + 2 < zn:
            scatter2.merge_side(k + 2)
    scatter2.merge_core(0, 1)
    scatter2.merge_core(0, 0)
    scatter2.merge_side(1)
    scatter2.merge_side(0)
    prediction = scatter2.result() * feature_norm
    res2[own, :] = (prediction - y_ref[...].astype(F32)).astype(BF16)
    gather2 = Gather(place, res2, rows, g_recv.at[2], g_send.at[2])
    scaled_ref[...] = descend(gather2, res2, out_ref)

    for transfer in (gather_x, scatter1, gather1, scatter2, gather2):
        transfer.finish()


def local(samples, targets, frequencies, phases, coefficients, eigenbasis, eigenvalues):
    size = lax.axis_size("feat")
    rows, din = samples.shape
    feat_dev = frequencies.shape[1]
    outs = coefficients.shape[1]
    top = eigenbasis.shape[1]
    zn = size // 4
    wide = outs + top
    total_rows = rows * size

    def scatter_buffers(columns):
        return [
            pltpu.VMEM((2 * zn, rows, columns), F32),
            pltpu.VMEM((2 * zn, rows, columns), BF16),
            pltpu.VMEM((2 * zn, rows, columns), BF16),
            pltpu.VMEM((zn, rows, columns), BF16),
            pltpu.VMEM((zn, rows, columns), BF16),
            pltpu.VMEM((zn, rows, columns), BF16),
            pltpu.VMEM((zn, rows, columns), BF16),
        ]

    vmem = pl.BlockSpec(memory_space=pltpu.VMEM)
    return pl.pallas_call(
        functools.partial(kernel, size, feat_dev * size),
        out_shape=(
            jax.ShapeDtypeStruct(coefficients.shape, F32),
            jax.ShapeDtypeStruct((top, outs), F32),
        ),
        in_specs=[vmem] * 7,
        out_specs=(vmem, vmem),
        scratch_shapes=[
            pltpu.VMEM((total_rows, din), BF16),
            pltpu.VMEM((total_rows, feat_dev), BF16),
            pltpu.VMEM((16, feat_dev), F32),
            pltpu.VMEM((feat_dev, wide), BF16),
            pltpu.VMEM((feat_dev, outs), BF16),
            pltpu.VMEM((feat_dev, outs), F32),
            pltpu.VMEM((2 * rows, wide), F32),
            pltpu.VMEM((total_rows, wide), BF16),
            pltpu.VMEM((total_rows, outs), BF16),
            *scatter_buffers(wide),
            *scatter_buffers(outs),
            pltpu.SemaphoreType.DMA((3, size)),
            pltpu.SemaphoreType.DMA((3, 5 * zn)),
            pltpu.SemaphoreType.DMA((2, 2, 2 * zn)),
            pltpu.SemaphoreType.DMA((2, 2, zn)),
            pltpu.SemaphoreType.DMA((2, 2, zn)),
        ],
        compiler_params=pltpu.CompilerParams(
            collective_id=0, has_side_effects=True, vmem_limit_bytes=60 * 1024 * 1024
        ),
    )(
        samples, targets, frequencies, phases.reshape(1, feat_dev), coefficients, eigenbasis,
        eigenvalues.reshape(1, top),
    )


def solution(mesh):
    return jax.shard_map(
        local,
        mesh=mesh,
        in_specs=(
            P(("groups", "feat"), None),
            P(("groups", "feat"), None),
            P(None, "feat"),
            P("feat"),
            P("feat", "groups"),
            P("feat", "groups"),
            P("groups"),
        ),
        out_specs=(P("feat", "groups"), P("groups", None)),
        check_vma=False,
    )
```

```python
import functools
import math

import jax
import jax.numpy as jnp
from jax import lax
from jax.experimental import pallas as pl
from jax.experimental.pallas import tpu as pltpu
from jax.sharding import PartitionSpec as P

STEPS = 2
F32 = jnp.float32
BF16 = jnp.bfloat16
COSINE = (
    0.9999991998413434, -19.738978175861273, 64.92858783993262,
    -85.27084362689533, 58.786940762944745, -21.065429407375632,
)
TN_DIMS = (((0,), (0,)), ((), ()))


def tn_dot(left, right):
    return lax.dot_general(left, right, TN_DIMS, preferred_element_type=F32)


class Gather:
    def __init__(self, place, buf, rows, recv, send):
        self.place, self.buf, self.rows, self.recv, self.send = place, buf, rows, recv, send

    def copy(self, chunk, slot, target):
        part = self.buf.at[pl.ds(pl.multiple_of(chunk * self.rows, self.rows), self.rows)]
        return pltpu.make_async_remote_copy(
            src_ref=part,
            dst_ref=part,
            send_sem=self.send.at[slot],
            recv_sem=self.recv.at[chunk],
            device_id={"feat": target},
            device_id_type=pl.DeviceIdType.MESH,
        )

    def arrived(self, chunk):
        self.copy(chunk, 0, self.place.sibling).wait_recv()

    def line_copies(self, k):
        s = self.place
        chunk = s.chunk(k, s.y, s.c)
        right = (s.q + 1 < s.zn) if k == 0 else jnp.logical_and(s.order[k] < s.q, s.q + 1 < s.zn)
        left = (s.q > 0) if k == 0 else jnp.logical_and(s.order[k] > s.q, s.q > 0)
        return (
            (right, self.copy(chunk, 5 * k, s.device(jnp.minimum(s.q + 1, s.zn - 1), s.y, s.c))),
            (left, self.copy(chunk, 5 * k + 1, s.device(jnp.maximum(s.q - 1, 0), s.y, s.c))),
        )

    def near_copies(self, k):
        s = self.place
        chunk = s.chunk(k, s.y, s.c)
        return (self.copy(chunk, 5 * k + 2, s.partner), self.copy(chunk, 5 * k + 3, s.sibling))

    def cross_copy(self, k):
        s = self.place
        return self.copy(s.chunk(k, 1 - s.y, s.c), 5 * k + 4, s.sibling)

    def forward(self, k):
        s = self.place
        if k > 0:
            self.arrived(s.chunk(k, s.y, s.c))
        for needed, copy in self.line_copies(k):
            pl.when(needed)(copy.start)
        for copy in self.near_copies(k):
            copy.start()

    def cross(self, k):
        s = self.place
        self.arrived(s.chunk(k, 1 - s.y, s.c))
        self.cross_copy(k).start()

    def near_half(self, k):
        s = self.place
        self.arrived(s.chunk(k, s.y, 1 - s.c))

    def far_half(self, k):
        s = self.place
        self.arrived(s.chunk(k, 1 - s.y, 1 - s.c))

    def finish(self):
        for k in range(self.place.zn):
            for needed, copy in self.line_copies(k):
                pl.when(needed)(copy.wait_send)
            for copy in self.near_copies(k):
                copy.wait_send()
            self.cross_copy(k).wait_send()


class Scatter:
    def __init__(self, place, rows, keep, core, side, line, core_sem, side_sem, line_sem):
        self.place, self.rows = place, rows
        self.keep = keep
        self.core_out, self.core_in = core
        self.side_out, self.side_in = side
        self.line_out, self.line_in = line
        self.core_sem, self.side_sem, self.line_sem = core_sem, side_sem, line_sem

    def core_copy(self, slot):
        return pltpu.make_async_remote_copy(
            src_ref=self.core_out.at[slot],
            dst_ref=self.core_in.at[slot],
            send_sem=self.core_sem.at[0, slot],
            recv_sem=self.core_sem.at[1, slot],
            device_id={"feat": self.place.sibling},
            device_id_type=pl.DeviceIdType.MESH,
        )

    def side_copy(self, k):
        return pltpu.make_async_remote_copy(
            src_ref=self.side_out.at[k],
            dst_ref=self.side_in.at[k],
            send_sem=self.side_sem.at[0, k],
            recv_sem=self.side_sem.at[1, k],
            device_id={"feat": self.place.partner},
            device_id_type=pl.DeviceIdType.MESH,
        )

    def line_copy(self, k):
        s = self.place
        return pltpu.make_async_remote_copy(
            src_ref=self.line_out.at[k],
            dst_ref=self.line_in.at[s.q],
            send_sem=self.line_sem.at[0, k],
            recv_sem=self.line_sem.at[1, s.q],
            device_id={"feat": s.device(s.order[k], s.y, s.c)},
            device_id_type=pl.DeviceIdType.MESH,
        )

    def line_arrival(self, k):
        s = self.place
        other = s.order[k]
        return pltpu.make_async_remote_copy(
            src_ref=self.line_out.at[k],
            dst_ref=self.line_in.at[other],
            send_sem=self.line_sem.at[0, k],
            recv_sem=self.line_sem.at[1, other],
            device_id={"feat": s.device(other, s.y, s.c)},
            device_id_type=pl.DeviceIdType.MESH,
        )

    def put(self, k, far, sums):
        slot = 2 * k + far
        self.keep[slot] = sums(self.place.c)
        self.core_out[slot] = sums(1 - self.place.c).astype(BF16)
        self.core_copy(slot).start()

    def merge_core(self, k, far):
        slot = 2 * k + far
        self.core_copy(slot).wait_recv()
        total = self.keep[slot] + self.core_in[slot].astype(F32)
        if far:
            self.side_out[k] = total.astype(BF16)
            self.side_copy(k).start()
        else:
            self.keep[slot] = total

    def merge_side(self, k):
        self.side_copy(k).wait_recv()
        total = self.keep[2 * k] + self.side_in[k].astype(F32)
        if k:
            self.line_out[k] = total.astype(BF16)
            self.line_copy(k).start()
        else:
            self.keep[0] = total

    def result(self):
        total = self.keep[0]
        for k in range(1, self.place.zn):
            self.line_arrival(k).wait_recv()
            total = total + self.line_in[self.place.order[k]].astype(F32)
        return total

    def finish(self):
        for k in range(self.place.zn):
            self.core_copy(2 * k).wait_send()
            self.core_copy(2 * k + 1).wait_send()
            self.side_copy(k).wait_send()
            if k:
                self.line_copy(k).wait_send()


class Place:
    def __init__(self, size):
        self.zn = zn = size // 4
        me = lax.axis_index("feat")
        self.me = me
        self.q = q = me // 4
        self.y = (me // 2) % 2
        self.c = me % 2
        near = jnp.minimum(q, zn - 1 - q)
        self.order = []
        for k in range(zn):
            step = -((k + 1) // 2) if k % 2 else k // 2
            edge = jnp.where(q == near, k, zn - 1 - k)
            self.order.append(jnp.where(k <= 2 * near, q + step, edge))
        self.sibling = self.device(q, self.y, 1 - self.c)
        self.partner = self.device(q, 1 - self.y, self.c)

    def device(self, q, y, c):
        return (q * 2 + y) * 2 + c

    def chunk(self, k, y, c):
        return self.device(self.order[k], y, c)


def kernel(
    size, total_feat,
    x_ref, y_ref, w_ref, phase_ref, a_ref, e_ref, eig_ref,
    out_ref, scaled_ref,
    xs, feats, spread, joint, low, grad, part, res1, res2,
    keep1, core_out1, core_in1, side_out1, side_in1, line_out1, line_in1,
    keep2, core_out2, core_in2, side_out2, side_in2, line_out2, line_in2,
    g_recv, g_send, s_core, s_side, s_line,
):
    place = Place(size)
    zn = place.zn
    rows = x_ref.shape[0]
    feat_dev = w_ref.shape[1]
    outs = a_ref.shape[1]
    top = e_ref.shape[1]
    tile = min(256, feat_dev)
    tiles = feat_dev // tile
    total_rows = rows * size
    step_rate = 0.5 * math.sqrt(total_rows / total_feat)
    feature_norm = 1.0 / math.sqrt(total_feat)
    sample_norm = 1.0 / math.sqrt(total_rows)

    barrier = pltpu.get_barrier_semaphore()
    others = [place.sibling, place.partner] + [
        place.device(place.order[k], place.y, place.c) for k in range(1, zn)
    ]
    for other in others:
        pl.semaphore_signal(
            barrier, inc=1, device_id={"feat": other}, device_id_type=pl.DeviceIdType.MESH
        )

    own = pl.ds(pl.multiple_of(place.me * rows, rows), rows)
    xs[own, :] = x_ref[...]
    pl.semaphore_wait(barrier, len(others))
    gather_x = Gather(place, xs, rows, g_recv.at[0], g_send.at[0])
    gather_x.forward(0)

    index = (place.me * feat_dev + lax.broadcasted_iota(jnp.int32, (8, feat_dev), 1)).astype(F32)
    turn = 1.0 / (2.0 * math.pi)
    sweep = jnp.exp(F32(math.log(8.0)) * index / F32(total_feat))
    spread[0:8, :] = sweep * turn
    spread[8:16, :] = jnp.broadcast_to(phase_ref[...] * turn, (8, feat_dev))
    joint[:, :outs] = a_ref[...].astype(BF16)
    joint[:, outs:] = e_ref[...]

    pair = 2 * rows

    def pair_rows(k, far):
        y = 1 - place.y if far else place.y
        first = (place.order[k] * 2 + y) * pair
        return pl.ds(pl.multiple_of(first, pair), pair)

    def make_features(span, halfway=None):
        def body(i, carry):
            cols = pl.ds(pl.multiple_of(i * tile, tile), tile)
            product = jnp.dot(xs[span, :], w_ref[:, cols], preferred_element_type=F32)
            turns = product * spread[0:1, cols] + spread[8:9, cols]
            f = turns - jnp.round(turns)
            u = f * f
            value = jnp.full_like(u, COSINE[-1])
            for coefficient in COSINE[-2::-1]:
                value = value * u + coefficient
            feats[span, cols] = value.astype(BF16)
            return carry

        middle = tiles // 2
        lax.fori_loop(0, middle, body, 0, unroll=True)
        if halfway is not None:
            halfway()
        lax.fori_loop(middle, tiles, body, 0, unroll=True)

    def predict(span, factors, scatter, k, far, columns):
        part[:, :columns] = jnp.dot(feats[span, :], factors[...], preferred_element_type=F32)

        def sums(core):
            return part[pl.ds(pl.multiple_of(core * rows, rows), rows), :columns]

        scatter.put(k, far, sums)

    scatter1 = Scatter(
        place, rows, keep1, (core_out1, core_in1), (side_out1, side_in1), (line_out1, line_in1),
        s_core.at[0], s_side.at[0], s_line.at[0],
    )
    scatter2 = Scatter(
        place, rows, keep2, (core_out2, core_in2), (side_out2, side_in2), (line_out2, line_in2),
        s_core.at[1], s_side.at[1], s_line.at[1],
    )

    for k in range(zn):
        gather_x.near_half(k)

        def halfway(k=k):
            if k + 1 < zn:
                gather_x.forward(k + 1)

        make_features(pair_rows(k, 0), halfway)
        gather_x.cross(k)
        predict(pair_rows(k, 0), joint, scatter1, k, 0, outs + top)
        if k:
            scatter1.merge_core(k - 1, 1)
        gather_x.far_half(k)
        make_features(pair_rows(k, 1))
        scatter1.merge_core(k, 0)
        predict(pair_rows(k, 1), joint, scatter1, k, 1, outs + top)
        if k:
            scatter1.merge_side(k - 1)
    scatter1.merge_core(zn - 1, 1)
    scatter1.merge_side(zn - 1)

    total = scatter1.result()
    prediction = total[:, :outs] * feature_norm
    res1[own, :outs] = (prediction - y_ref[...].astype(F32)).astype(BF16)
    res1[own, outs:] = total[:, outs:].astype(BF16)

    eig = jnp.broadcast_to(1.0 - 1.0 / eig_ref[...], (top, top))
    same = lax.broadcasted_iota(jnp.int32, (top, top), 0) == lax.broadcasted_iota(
        jnp.int32, (top, top), 1
    )
    retained = jnp.sum(jnp.where(same, eig, 0.0), axis=1, keepdims=True)

    def descend(gather, res, source):
        quad = 4 * rows
        projected = jnp.zeros((top, outs), F32)
        gather.forward(0)
        gather.forward(1)
        for k in range(zn):
            gather.cross(k)
            if k + 2 < zn:
                gather.forward(k + 2)
            gather.near_half(k)
            gather.far_half(k)
            span = pl.ds(pl.multiple_of(place.order[k] * quad, quad), quad)

            def body(i, carry):
                cols = pl.ds(pl.multiple_of(i * tile, tile), tile)
                term = tn_dot(feats[span, cols], res[span, :outs])
                grad[cols, :] = term if k == 0 else grad[cols, :] + term
                return carry

            lax.fori_loop(0, tiles, body, 0, unroll=True)
            projected = projected + tn_dot(res1[span, outs:], res[span, :outs])
        scaled = retained * (projected * sample_norm)
        upper = scaled.astype(BF16)
        lower = (scaled - upper.astype(F32)).astype(BF16)

        def update(i, carry):
            cols = pl.ds(pl.multiple_of(i * tile, tile), tile)
            basis = e_ref[cols, :]
            correction = jnp.dot(basis, upper, preferred_element_type=F32) + jnp.dot(
                basis, lower, preferred_element_type=F32
            )
            new = source[cols, :] - step_rate * (grad[cols, :] * sample_norm - correction)
            out_ref[cols, :] = new
            low[cols, :] = new.astype(BF16)
            return carry

        lax.fori_loop(0, tiles, update, 0)
        return scaled

    gather1 = Gather(place, res1, rows, g_recv.at[1], g_send.at[1])
    descend(gather1, res1, a_ref)

    for k in reversed(range(zn)):
        for far in (1, 0):
            predict(pair_rows(k, far), low, scatter2, k, far, outs)
        if k + 1 < zn:
            scatter2.merge_core(k + 1, 1)
            scatter2.merge_core(k + 1, 0)
        if k + 2 < zn:
            scatter2.merge_side(k + 2)
    scatter2.merge_core(0, 1)
    scatter2.merge_core(0, 0)
    scatter2.merge_side(1)
    scatter2.merge_side(0)
    prediction = scatter2.result() * feature_norm
    res2[own, :] = (prediction - y_ref[...].astype(F32)).astype(BF16)
    gather2 = Gather(place, res2, rows, g_recv.at[2], g_send.at[2])
    scaled_ref[...] = descend(gather2, res2, out_ref)

    for transfer in (gather_x, scatter1, gather1, scatter2, gather2):
        transfer.finish()


def local(samples, targets, frequencies, phases, coefficients, eigenbasis, eigenvalues):
    size = lax.axis_size("feat")
    rows, din = samples.shape
    feat_dev = frequencies.shape[1]
    outs = coefficients.shape[1]
    top = eigenbasis.shape[1]
    zn = size // 4
    wide = outs + top
    total_rows = rows * size

    def scatter_buffers(columns):
        return [
            pltpu.VMEM((2 * zn, rows, columns), F32),
            pltpu.VMEM((2 * zn, rows, columns), BF16),
            pltpu.VMEM((2 * zn, rows, columns), BF16),
            pltpu.VMEM((zn, rows, columns), BF16),
            pltpu.VMEM((zn, rows, columns), BF16),
            pltpu.VMEM((zn, rows, columns), BF16),
            pltpu.VMEM((zn, rows, columns), BF16),
        ]

    vmem = pl.BlockSpec(memory_space=pltpu.VMEM)
    return pl.pallas_call(
        functools.partial(kernel, size, feat_dev * size),
        out_shape=(
            jax.ShapeDtypeStruct(coefficients.shape, F32),
            jax.ShapeDtypeStruct((top, outs), F32),
        ),
        in_specs=[vmem] * 7,
        out_specs=(vmem, vmem),
        scratch_shapes=[
            pltpu.VMEM((total_rows, din), BF16),
            pltpu.VMEM((total_rows, feat_dev), BF16),
            pltpu.VMEM((16, feat_dev), F32),
            pltpu.VMEM((feat_dev, wide), BF16),
            pltpu.VMEM((feat_dev, outs), BF16),
            pltpu.VMEM((feat_dev, outs), F32),
            pltpu.VMEM((2 * rows, wide), F32),
            pltpu.VMEM((total_rows, wide), BF16),
            pltpu.VMEM((total_rows, outs), BF16),
            *scatter_buffers(wide),
            *scatter_buffers(outs),
            pltpu.SemaphoreType.DMA((3, size)),
            pltpu.SemaphoreType.DMA((3, 5 * zn)),
            pltpu.SemaphoreType.DMA((2, 2, 2 * zn)),
            pltpu.SemaphoreType.DMA((2, 2, zn)),
            pltpu.SemaphoreType.DMA((2, 2, zn)),
        ],
        compiler_params=pltpu.CompilerParams(
            collective_id=0, has_side_effects=True, vmem_limit_bytes=60 * 1024 * 1024
        ),
    )(
        samples, targets, frequencies, phases.reshape(1, feat_dev), coefficients, eigenbasis,
        eigenvalues.reshape(1, top),
    )


def solution(mesh):
    return jax.shard_map(
        local,
        mesh=mesh,
        in_specs=(
            P(("groups", "feat"), None),
            P(("groups", "feat"), None),
            P(None, "feat"),
            P("feat"),
            P("feat", "groups"),
            P("feat", "groups"),
            P("groups"),
        ),
        out_specs=(P("feat", "groups"), P("groups", None)),
        check_vma=False,
    )
```
